256 devices in a mesh: row: 32 (over x, z_hi, core), walk: 8 (over y, z_lo).
Axes of the slice: x: 4, y: 4, z: 8 (z_hi: 4, z_lo: 2; z = z_hi * 2 + z_lo), core: 2. Of those that a mesh axis runs over, the one named last changes fastest.
Arguments:
- cholesky: bfloat16 [256, 1024, 1024], P(None, 'row'), may hold values from -0.125 to 0.125
- walkers: bfloat16 [256, 1024, 256], P('walk', 'row'), may hold values from -6 to 6
- trial_orbitals: bfloat16 [1024, 256], P('row'), may hold values from -0.015625 to 0.015625
- fields: float32 [2, 256, 256], P(None, 'walk'), may hold values from -6 to 6
- log_weights: float32 [256], P('walk'), may hold values from -1.2 to 2.4
Outputs:
- walkers_out: bfloat16 [256, 1024, 256], P('walk', 'row')
- log_weights_out: float32 [256], P('walk')
The draws below stay inside these ranges and needn't reach their ends.
All inputs are finite; a program needn't handle non-finite values.
Results may differ from the reference program's by a relative error of at most 0.025.
Values may be sent and summed in bfloat16 or wider, within the bound.
No kernel may reach another device: no remote copies, remote signals or barrier semaphores. Data moves between devices by JAX's collectives and lax.ppermute only.
A program may use at most 128 MiB of HBM per device.

```python
import jax
import jax.numpy as jnp
from jax import lax

N = 1024
NE = 256
NG = 256
STEPS = 2
W_ALL = 256


def draw_log_weights(key, part):
    key = jax.random.fold_in(key, 7)
    position = jnp.arange(W_ALL, dtype=jnp.float32)
    ramp = jnp.log(1.0 + 2.0 * position / (W_ALL - 1))
    noise = jax.random.uniform(key, (W_ALL,), jnp.float32, -0.5, 0.5)
    return noise + ramp


def shard_levels(key, extent, shards, smallest, high):
    def one(axis_at, blocks):
        heights = jax.random.uniform(jax.random.fold_in(jax.random.fold_in(key, 6), axis_at), (blocks,), jnp.float32, smallest / len(shards), high / len(shards))
        return jnp.repeat(jnp.exp(heights), extent[axis_at] // blocks).reshape((-1,) + (1,) * (len(extent) - axis_at - 1))

    factor_of = one(*shards[0])
    for cut in shards[1:]:
        factor_of = factor_of * one(*cut)
    return factor_of


def scatter_about(own_key, extent, width, limit, split=(), held_as=jnp.bfloat16):
    loudness = shard_levels(own_key, extent, split, -0.22, 0.18) if split else 1.0
    values = jax.random.normal(own_key, extent, jnp.float32) * width * loudness
    return jnp.minimum(jnp.maximum(values, -limit), limit).astype(held_as)


def setup_inputs(seed: int = 0) -> dict:
    seeds = jax.random.split(jax.random.key(seed), 6)
    return {
        "cholesky": scatter_about(seeds[0], (NG, N, N), (11.0 / (N * NG) ** 0.5), 0.125, ((1, 32),)),
        "walkers": scatter_about(seeds[1], (W_ALL, N, NE), 1.0, 6.0, ((0, 8), (1, 32))),
        "trial_orbitals": scatter_about(seeds[2], (N, NE), (0.09 * (NG / (N * NE)) ** 0.5), 0.015625, ((0, 32),)),
        "fields": scatter_about(seeds[3], (STEPS, W_ALL, NG), 1.0, 6.0, ((1, 8),), jnp.float32),
        "log_weights": draw_log_weights(jax.random.fold_in(seeds[5], 71), 0),
    }


time_root = 0.1


def reference(cholesky, walkers, trial_orbitals, fields, log_weights):
    vectors = cholesky.astype(jnp.float32)
    rotated = jnp.einsum("gik,ke->gie", vectors, trial_orbitals.astype(jnp.float32)).astype(jnp.bfloat16)
    rotated_wide = rotated.astype(jnp.float32)
    current = walkers
    weights_now = log_weights
    for turn_index in range(STEPS):
        force_bias = jnp.einsum("wie,gie->wg", current.astype(jnp.float32), rotated_wide)
        shifted = time_root * force_bias
        aux_field = fields[turn_index]
        weights_now = weights_now + jnp.sum(aux_field * shifted - 0.5 * shifted * shifted, axis=1)
        mixed = lax.optimization_barrier((aux_field - shifted).astype(jnp.bfloat16)).astype(jnp.float32)

        def advance(operands):
            coeffs, walker = operands
            potential = (time_root * jnp.einsum("g,gik->ik", coeffs, vectors)).astype(jnp.bfloat16)
            summed = walker.astype(jnp.float32)
            power_term = walker
            for degree in range(1, 5):
                next_term = jnp.dot(potential, power_term, preferred_element_type=jnp.float32) / degree
                summed = summed + next_term
                power_term = next_term.astype(jnp.bfloat16)
            return summed.astype(jnp.bfloat16)

        current = lax.map(advance, (mixed, current))
    mean_weight = jnp.sum(jnp.exp(weights_now)) / W_ALL
    return current, weights_now - jnp.log(mean_weight)
```

```python
import jax
import jax.numpy as jnp
from jax import lax
from jax.sharding import Mesh, PartitionSpec as P

ROW = ("x", "zh", "c")
WALK = ("y", "zl")
time_root = 0.1


def exchange(value, axis):
    return lax.all_to_all(value, axis, split_axis=0, concat_axis=0, tiled=True)


def swap(value, axis):
    return lax.ppermute(value, axis, [(0, 1), (1, 0)])


def spread(value, axis):
    count = lax.axis_size(axis)
    return exchange(jnp.broadcast_to(value[None], (count,) + value.shape), axis)


def row_sum(part):
    core = lax.axis_index("c")
    count = part.shape[0] // 2
    halves = part.reshape((2, count) + part.shape[1:])
    mine = lax.dynamic_index_in_dim(halves, core, 0, False)
    other = lax.dynamic_index_in_dim(halves, 1 - core, 0, False)
    total = mine + swap(other, "c")
    total = jnp.sum(spread(total, ("x", "zh")), axis=0)
    other = swap(total, "c")
    return jnp.where(
        core == 0,
        jnp.concatenate([total, other]),
        jnp.concatenate([other, total]),
    )


def walk_sum(value):
    value = jnp.full((8, 128), value)
    value = value + swap(value, "zl")
    total = value
    for shift in range(1, 4):
        total = total + lax.ppermute(value, "y", [(i, (i + shift) % 4) for i in range(4)])
    return total[0, 0]


def taylor(potential, walker):
    summed = walker.astype(jnp.float32)
    power_term = walker
    for degree in range(1, 5):
        next_term = jnp.dot(potential, power_term, preferred_element_type=jnp.float32) / degree
        summed = summed + next_term
        power_term = next_term.astype(jnp.bfloat16)
    return summed.astype(jnp.bfloat16)


def shards(cholesky, walkers, trial_orbitals, fields, log_weights):
    vectors, rows, orbitals = cholesky.shape
    walker_count, _, electrons = walkers.shape
    trial = spread(trial_orbitals, ROW).reshape(orbitals, electrons)
    phi = exchange(walkers, ROW).reshape(orbitals, electrons)
    by_row = lax.optimization_barrier(jnp.swapaxes(cholesky, 0, 1))
    rotated = jnp.einsum("igk,ke->ige", by_row, trial, preferred_element_type=jnp.float32).astype(jnp.bfloat16)
    phi_rows = walkers
    weights_now = log_weights
    for step in range(fields.shape[0]):
        part = jnp.einsum("wie,ige->wg", phi_rows, rotated, preferred_element_type=jnp.float32)
        shifted = time_root * row_sum(part)
        aux_field = fields[step]
        weights_now = weights_now + jnp.sum(aux_field * shifted - 0.5 * shifted * shifted, axis=1)
        mixed = (aux_field - shifted).astype(jnp.bfloat16)
        potential = (
            time_root * jnp.einsum("wg,igk->wik", mixed, by_row, preferred_element_type=jnp.float32)
        ).astype(jnp.bfloat16)
        potential = exchange(potential, ROW).reshape(orbitals, orbitals)
        phi = taylor(potential, phi)
        phi_rows = exchange(phi.reshape(walker_count, rows, electrons), ROW)
    weight_sum = walk_sum(jnp.sum(jnp.exp(weights_now)))
    count = walker_count * lax.axis_size(WALK)
    return phi_rows, weights_now - jnp.log(weight_sum / count)


def solution(mesh):
    split = Mesh(mesh.devices.reshape(4, 4, 2, 4, 2), ROW + WALK)
    placed = (
        P(None, ROW, None),
        P(WALK, ROW, None),
        P(ROW, None),
        P(None, WALK, None),
        P(WALK),
    )
    return jax.shard_map(
        shards,
        mesh=split,
        in_specs=placed,
        out_specs=(P(WALK, ROW, None), P(WALK)),
        check_vma=False,
    )
```

```python
import functools

import jax
import jax.numpy as jnp
from jax import lax
from jax.experimental import pallas as pl
from jax.experimental.pallas import tpu as pltpu
from jax.sharding import Mesh, PartitionSpec as P

ROW = ("x", "zh", "c")
WALK = ("y", "zl")

block_rows = 8
time_root = 0.1
WHOLE = pl.BlockSpec(memory_space=pltpu.VMEM)
IN_HBM = pl.BlockSpec(memory_space=pltpu.HBM)
LAST = (((1,), (1,)), ((), ()))


def params(mebibytes):
    return pltpu.CompilerParams(vmem_limit_bytes=mebibytes * 2**20)


def cost(flops, size):
    return pl.CostEstimate(flops=flops, bytes_accessed=size, transcendentals=0)


def dot(left, right, dims=(((1,), (0,)), ((), ())), precision=None):
    return lax.dot_general(left, right, dims, precision=precision, preferred_element_type=jnp.float32)


def diagonal(walkers):
    shape = (1, block_rows, walkers * block_rows)
    lane = lax.broadcasted_iota(jnp.int32, shape, 2) % block_rows
    return lane == lax.broadcasted_iota(jnp.int32, shape, 1)


def reduce_diagonal(cross, walkers):
    kept = jnp.sum(jnp.where(diagonal(walkers), cross, 0.0), axis=1)
    shape = (walkers, walkers * block_rows)
    lane = lax.broadcasted_iota(jnp.int32, shape, 1) // block_rows
    pick = (lane == lax.broadcasted_iota(jnp.int32, shape, 0)).astype(jnp.float32)
    return dot(pick, kept, LAST, precision=lax.Precision.HIGHEST)


def diagonal(walkers):
    shape = (1, block_rows, walkers * block_rows)
    lane = lax.broadcasted_iota(jnp.int32, shape, 2) % block_rows
    return lane == lax.broadcasted_iota(jnp.int32, shape, 1)


def reduce_diagonal(cross, walkers):
    kept = jnp.sum(jnp.where(diagonal(walkers), cross, 0.0), axis=1)
    shape = (walkers, walkers * block_rows)
    lane = lax.broadcasted_iota(jnp.int32, shape, 1) // block_rows
    pick = (lane == lax.broadcasted_iota(jnp.int32, shape, 0)).astype(jnp.float32)
    return dot(pick, kept, LAST, precision=lax.Precision.HIGHEST)


def in_vmem(value):
    return pltpu.with_memory_space_constraint(value, pltpu.VMEM)


def pieces(vectors, rows):
    some = 512 // block_rows
    return [
        (slice(low, low + some), slice(start, start + block_rows))
        for low in range(0, vectors, some)
        for start in range(0, rows, block_rows)
    ]


def add_diagonal(rotated, phi_ref, at, some, cross_ref):
    right = phi_ref[:, at, :].reshape(-1, phi_ref.shape[2])
    cross = dot(rotated, right, LAST).reshape(-1, block_rows, right.shape[0])
    if at.start:
        cross = cross + cross_ref[some]
    cross_ref[some] = cross


def bias_kernel(rotated_ref, phi_ref, part_ref, cross_ref):
    vectors, rows, electrons = rotated_ref.shape
    for some, at in pieces(vectors, rows):
        add_diagonal(rotated_ref[some, at, :].reshape(-1, electrons), phi_ref, at, some, cross_ref)
    part_ref[...] = reduce_diagonal(cross_ref[...], phi_ref.shape[0])


def bias(rotated, phi):
    vectors = rotated.shape[0]
    walkers = phi.shape[0]
    return pl.pallas_call(
        bias_kernel,
        in_specs=[WHOLE] * 2,
        out_specs=WHOLE,
        out_shape=jax.ShapeDtypeStruct((walkers, vectors), jnp.float32),
        scratch_shapes=[pltpu.VMEM((vectors, block_rows, walkers * block_rows), jnp.float32)],
        compiler_params=params(12),
        cost_estimate=cost(2**30, 2**22),
    )(rotated, phi)


def fetch(chol_hbm, chol_ref, arrived):
    vectors, rows, _ = chol_ref.shape
    half = vectors // 2
    copies = {}
    for start in range(0, rows, block_rows):
        for low in range(0, vectors, half):
            at = (slice(low, low + half), slice(start, start + block_rows))
            copy = pltpu.make_async_copy(chol_hbm.at[at], chol_ref.at[at], arrived.at[len(copies)])
            copy.start()
            copies[start, low] = copy
    return copies


def first_bias_kernel(chol_hbm, trial_ref, phi_ref, part_ref, chol_ref, paired_ref, cross_ref, arrived):
    vectors, rows, orbitals = chol_ref.shape
    incoming = fetch(chol_hbm, chol_ref, arrived)
    for start in range(0, rows, block_rows):
        phi = phi_ref[:, start : start + block_rows, :].reshape(-1, phi_ref.shape[2])
        paired_ref[start // block_rows] = dot(phi, trial_ref[...], LAST).astype(jnp.bfloat16)
    some = 512 // block_rows
    for start in range(0, rows, block_rows):
        for low in range(0, vectors, some):
            if (start, low) in incoming:
                incoming[start, low].wait()
            piece = chol_ref[low : low + some, start : start + block_rows, :].reshape(-1, orbitals)
            cross = dot(piece, paired_ref[start // block_rows], LAST).reshape(some, block_rows, -1)
            if start:
                cross = cross + cross_ref[low : low + some]
            cross_ref[low : low + some] = cross
    part_ref[...] = reduce_diagonal(cross_ref[...], phi_ref.shape[0])


def first_bias(chol, trial, phi):
    vectors, rows, orbitals = chol.shape
    walkers = phi.shape[0]
    blocks = rows // block_rows
    wide = walkers * block_rows
    return pl.pallas_call(
        first_bias_kernel,
        in_specs=[IN_HBM, WHOLE, WHOLE],
        out_specs=WHOLE,
        out_shape=jax.ShapeDtypeStruct((walkers, vectors), jnp.float32),
        scratch_shapes=[
            pltpu.VMEM(chol.shape, chol.dtype),
            pltpu.VMEM((blocks, wide, orbitals), jnp.bfloat16),
            pltpu.VMEM((vectors, block_rows, wide), jnp.float32),
            pltpu.SemaphoreType.DMA((2 * blocks,)),
        ],
        compiler_params=params(50),
        cost_estimate=cost(2**32, 2**24),
    )(chol, trial, phi)


def rotate_kernel(chol_hbm, trial_ref, rotated_hbm, chol_ref, rotated_ref, arrived, left):
    vectors, rows, orbitals = chol_ref.shape
    electrons = trial_ref.shape[1]
    incoming = fetch(chol_hbm, chol_ref, arrived)
    outgoing = []
    for start in range(0, rows, block_rows):
        at = slice(start, start + block_rows)
        for low in range(0, vectors, 512 // block_rows):
            if (start, low) in incoming:
                incoming[start, low].wait()
            some = slice(low, low + 512 // block_rows)
            piece = chol_ref[some, at, :].reshape(-1, orbitals)
            rotated = dot(piece, trial_ref[...]).astype(jnp.bfloat16)
            rotated_ref[some, at, :] = rotated.reshape(-1, block_rows, electrons)
        copy = pltpu.make_async_copy(
            rotated_ref.at[:, at], rotated_hbm.at[:, at], left.at[start // block_rows]
        )
        copy.start()
        outgoing.append(copy)
    for copy in outgoing:
        copy.wait()


def rotate(chol, trial):
    vectors, rows, _ = chol.shape
    blocks = rows // block_rows
    shape = (vectors, rows, trial.shape[1])
    return pl.pallas_call(
        rotate_kernel,
        in_specs=[IN_HBM, WHOLE],
        out_specs=IN_HBM,
        out_shape=jax.ShapeDtypeStruct(shape, jnp.bfloat16),
        scratch_shapes=[
            pltpu.VMEM(chol.shape, chol.dtype),
            pltpu.VMEM(shape, jnp.bfloat16),
            pltpu.SemaphoreType.DMA((2 * blocks,)),
            pltpu.SemaphoreType.DMA((blocks,)),
        ],
        compiler_params=params(50),
        cost_estimate=cost(2**32, 2**24),
    )(chol, trial)


def potential_kernel(mixed_ref, chol_hbm, out_ref, wide_ref, chol_ref, arrived):
    walkers, vectors = mixed_ref.shape
    _, rows, orbitals = chol_ref.shape
    incoming = fetch(chol_hbm, chol_ref, arrived)
    keep = diagonal(256 // block_rows)
    g = lax.broadcasted_iota(jnp.int32, (vectors, 256), 0)
    lane = lax.broadcasted_iota(jnp.int32, (vectors, 256), 1) // block_rows
    for start in range(0, vectors * block_rows, 256):
        pick = (g == start // block_rows + lane).astype(jnp.bfloat16)
        wide = jnp.where(keep, dot(mixed_ref[...], pick)[:, None, :], 0.0)
        wide_ref[:, start : start + 256] = wide.reshape(-1, 256).astype(jnp.bfloat16)
    for start in range(0, rows, block_rows):
        at = slice(start, start + block_rows)
        incoming[start, 0].wait()
        incoming[start, vectors // 2].wait()
        for low in range(0, orbitals, 256):
            right = chol_ref[:, at, low : low + 256].reshape(vectors * block_rows, 256)
            out = time_root * dot(wide_ref[...], right)
            out_ref[:, at, low : low + 256] = out.astype(jnp.bfloat16).reshape(walkers, block_rows, 256)


def potential(mixed, chol):
    walkers, vectors = mixed.shape
    _, rows, orbitals = chol.shape
    return pl.pallas_call(
        potential_kernel,
        in_specs=[WHOLE, IN_HBM],
        out_specs=WHOLE,
        out_shape=jax.ShapeDtypeStruct((walkers, rows, orbitals), jnp.bfloat16),
        scratch_shapes=[
            pltpu.VMEM((walkers * block_rows, vectors * block_rows), jnp.bfloat16),
            pltpu.VMEM(chol.shape, chol.dtype),
            pltpu.SemaphoreType.DMA((2 * rows // block_rows,)),
        ],
        compiler_params=params(50),
    )(mixed, chol)


def exchange(value, axis):
    return lax.all_to_all(value, axis, split_axis=0, concat_axis=0, tiled=True)


def swap(value, axis):
    return lax.ppermute(value, axis, [(0, 1), (1, 0)])


def spread(value, axis):
    count = lax.axis_size(axis)
    return exchange(jnp.broadcast_to(value[None], (count,) + value.shape), axis)


def ring_sum(value, axis):
    total = value
    for shift in range(1, 4):
        total = total + lax.ppermute(value, axis, [(i, (i + shift) % 4) for i in range(4)])
    return total


def row_sum(part, by_permutes):
    core = lax.axis_index("c")
    count = part.shape[0] // 2
    halves = part.reshape((2, count) + part.shape[1:])
    mine = lax.dynamic_index_in_dim(halves, core, 0, False)
    other = lax.dynamic_index_in_dim(halves, 1 - core, 0, False)
    total = mine + swap(other, "c")
    if by_permutes:
        total = ring_sum(ring_sum(total, "x"), "zh")
    else:
        total = jnp.sum(spread(total, ("x", "zh")), axis=0)
    other = swap(total, "c")
    return jnp.where(
        core == 0,
        jnp.concatenate([total, other]),
        jnp.concatenate([other, total]),
    )


def gather_trial(rows):
    core = lax.axis_index("c")
    mine = spread(rows, ("x", "zh"))
    other = swap(mine, "c")
    both = jnp.where(core == 0, jnp.stack([mine, other], 1), jnp.stack([other, mine], 1))
    return both.reshape(-1, rows.shape[-1])


def taylor(potential, walker):
    summed = walker.astype(jnp.float32)
    power_term = walker
    for degree in range(1, 5):
        next_term = jnp.dot(potential, power_term, preferred_element_type=jnp.float32) / degree
        summed = summed + next_term
        power_term = next_term.astype(jnp.bfloat16)
    return summed.astype(jnp.bfloat16)


def shards(cholesky, walkers, trial_orbitals, fields, log_weights):
    vectors, rows, orbitals = cholesky.shape
    walker_count, _, electrons = walkers.shape
    trial = gather_trial(trial_orbitals)
    phi = exchange(walkers, ROW).reshape(orbitals, electrons)
    part = first_bias(cholesky, trial, walkers)
    weights_now = log_weights
    steps = fields.shape[0]
    for step in range(steps):
        shifted = time_root * row_sum(part, by_permutes=step == 0)
        aux_field = fields[step]
        weights_now = weights_now + jnp.sum(aux_field * shifted - 0.5 * shifted * shifted, axis=1)
        mixed = (aux_field - shifted).astype(jnp.bfloat16)
        sent = potential(mixed, cholesky)
        if step == 0:
            sent, trial, phi = lax.optimization_barrier((sent, trial, phi))
            rotated = rotate(cholesky, trial)
        if step == steps - 1:
            pair_sum = jnp.full((8, 128), jnp.sum(jnp.exp(weights_now)))
            pair_sum = pair_sum + swap(pair_sum, "zl")
            sent, pair_sum = lax.optimization_barrier((sent, pair_sum))
        sent = exchange(sent, ROW).reshape(orbitals, orbitals)
        if step == 0:
            sent, rotated = lax.optimization_barrier((sent, rotated))
        if step == steps - 1:
            weight_sum = ring_sum(pair_sum, "y")[0, 0]
            count = walker_count * lax.axis_size(WALK)
            weights_now = weights_now - jnp.log(weight_sum / count)
        phi = taylor(sent, phi)
        if step == steps - 1:
            phi, weights_now = lax.optimization_barrier((phi, weights_now))
        phi_rows = exchange(phi.reshape(walker_count, rows, electrons), ROW)
        if step < steps - 1:
            part = bias(rotated, phi_rows)
    return phi_rows, weights_now


def solution(mesh):
    split = Mesh(mesh.devices.reshape(4, 4, 2, 4, 2), ROW + WALK)
    placed = (
        P(None, ROW, None),
        P(WALK, ROW, None),
        P(ROW, None),
        P(None, WALK, None),
        P(WALK),
    )
    return jax.shard_map(
        shards,
        mesh=split,
        in_specs=placed,
        out_specs=(P(WALK, ROW, None), P(WALK)),
        check_vma=False,
    )
```

```python
import functools

import jax
import jax.numpy as jnp
from jax import lax
from jax.experimental import pallas as pl
from jax.experimental.pallas import tpu as pltpu
from jax.sharding import Mesh, PartitionSpec as P

ROW = ("x", "zh", "c")
WALK = ("y", "zl")

block_rows = 8
time_root = 0.1
WHOLE = pl.BlockSpec(memory_space=pltpu.VMEM)
IN_HBM = pl.BlockSpec(memory_space=pltpu.HBM)
LAST = (((1,), (1,)), ((), ()))


def params(mebibytes):
    return pltpu.CompilerParams(vmem_limit_bytes=mebibytes * 2**20)


def cost(flops, size):
    return pl.CostEstimate(flops=flops, bytes_accessed=size, transcendentals=0)


def dot(left, right, dims=(((1,), (0,)), ((), ())), precision=None):
    return lax.dot_general(left, right, dims, precision=precision, preferred_element_type=jnp.float32)


def diagonal(walkers):
    shape = (1, block_rows, walkers * block_rows)
    lane = lax.broadcasted_iota(jnp.int32, shape, 2) % block_rows
    return lane == lax.broadcasted_iota(jnp.int32, shape, 1)


def reduce_diagonal(cross, walkers):
    kept = jnp.sum(jnp.where(diagonal(walkers), cross, 0.0), axis=1)
    shape = (walkers, walkers * block_rows)
    lane = lax.broadcasted_iota(jnp.int32, shape, 1) // block_rows
    pick = (lane == lax.broadcasted_iota(jnp.int32, shape, 0)).astype(jnp.float32)
    return dot(pick, kept, LAST, precision=lax.Precision.HIGHEST)


def diagonal(walkers):
    shape = (1, block_rows, walkers * block_rows)
    lane = lax.broadcasted_iota(jnp.int32, shape, 2) % block_rows
    return lane == lax.broadcasted_iota(jnp.int32, shape, 1)


def reduce_diagonal(cross, walkers):
    kept = jnp.sum(jnp.where(diagonal(walkers), cross, 0.0), axis=1)
    shape = (walkers, walkers * block_rows)
    lane = lax.broadcasted_iota(jnp.int32, shape, 1) // block_rows
    pick = (lane == lax.broadcasted_iota(jnp.int32, shape, 0)).astype(jnp.float32)
    return dot(pick, kept, LAST, precision=lax.Precision.HIGHEST)


def in_vmem(value):
    return pltpu.with_memory_space_constraint(value, pltpu.VMEM)


def pieces(vectors, rows):
    some = 512 // block_rows
    return [
        (slice(low, low + some), slice(start, start + block_rows))
        for low in range(0, vectors, some)
        for start in range(0, rows, block_rows)
    ]


def add_diagonal(rotated, phi_ref, at, some, cross_ref):
    right = phi_ref[:, at, :].reshape(-1, phi_ref.shape[2])
    cross = dot(rotated, right, LAST).reshape(-1, block_rows, right.shape[0])
    if at.start:
        cross = cross + cross_ref[some]
    cross_ref[some] = cross


def bias_kernel(rotated_ref, phi_ref, part_ref, cross_ref):
    vectors, rows, electrons = rotated_ref.shape
    for some, at in pieces(vectors, rows):
        add_diagonal(rotated_ref[some, at, :].reshape(-1, electrons), phi_ref, at, some, cross_ref)
    part_ref[...] = reduce_diagonal(cross_ref[...], phi_ref.shape[0])


def bias(rotated, phi):
    vectors = rotated.shape[0]
    walkers = phi.shape[0]
    return pl.pallas_call(
        bias_kernel,
        in_specs=[WHOLE] * 2,
        out_specs=WHOLE,
        out_shape=jax.ShapeDtypeStruct((walkers, vectors), jnp.float32),
        scratch_shapes=[pltpu.VMEM((vectors, block_rows, walkers * block_rows), jnp.float32)],
        compiler_params=params(12),
        cost_estimate=cost(2**30, 2**22),
    )(rotated, phi)


def fetch(chol_hbm, chol_ref, arrived):
    vectors, rows, _ = chol_ref.shape
    half = vectors // 2
    copies = {}
    for start in range(0, rows, block_rows):
        for low in range(0, vectors, half):
            at = (slice(low, low + half), slice(start, start + block_rows))
            copy = pltpu.make_async_copy(chol_hbm.at[at], chol_ref.at[at], arrived.at[len(copies)])
            copy.start()
            copies[start, low] = copy
    return copies


def first_bias_kernel(chol_hbm, trial_ref, phi_ref, part_ref, chol_ref, paired_ref, cross_ref, arrived):
    vectors, rows, orbitals = chol_ref.shape
    incoming = fetch(chol_hbm, chol_ref, arrived)
    for start in range(0, rows, block_rows):
        phi = phi_ref[:, start : start + block_rows, :].reshape(-1, phi_ref.shape[2])
        paired_ref[start // block_rows] = dot(phi, trial_ref[...], LAST).astype(jnp.bfloat16)
    some = 512 // block_rows
    for start in range(0, rows, block_rows):
        for low in range(0, vectors, some):
            if (start, low) in incoming:
                incoming[start, low].wait()
            piece = chol_ref[low : low + some, start : start + block_rows, :].reshape(-1, orbitals)
            cross = dot(piece, paired_ref[start // block_rows], LAST).reshape(some, block_rows, -1)
            if start:
                cross = cross + cross_ref[low : low + some]
            cross_ref[low : low + some] = cross
    part_ref[...] = reduce_diagonal(cross_ref[...], phi_ref.shape[0])


def first_bias(chol, trial, phi):
    vectors, rows, orbitals = chol.shape
    walkers = phi.shape[0]
    blocks = rows // block_rows
    wide = walkers * block_rows
    return pl.pallas_call(
        first_bias_kernel,
        in_specs=[IN_HBM, WHOLE, WHOLE],
        out_specs=WHOLE,
        out_shape=jax.ShapeDtypeStruct((walkers, vectors), jnp.float32),
        scratch_shapes=[
            pltpu.VMEM(chol.shape, chol.dtype),
            pltpu.VMEM((blocks, wide, orbitals), jnp.bfloat16),
            pltpu.VMEM((vectors, block_rows, wide), jnp.float32),
            pltpu.SemaphoreType.DMA((2 * blocks,)),
        ],
        compiler_params=params(50),
        cost_estimate=cost(2**32, 2**24),
    )(chol, trial, phi)


def rotate_kernel(chol_hbm, trial_ref, rotated_hbm, chol_ref, rotated_ref, arrived, left):
    vectors, rows, orbitals = chol_ref.shape
    electrons = trial_ref.shape[1]
    incoming = fetch(chol_hbm, chol_ref, arrived)
    outgoing = []
    for start in range(0, rows, block_rows):
        at = slice(start, start + block_rows)
        for low in range(0, vectors, 512 // block_rows):
            if (start, low) in incoming:
                incoming[start, low].wait()
            some = slice(low, low + 512 // block_rows)
            piece = chol_ref[some, at, :].reshape(-1, orbitals)
            rotated = dot(piece, trial_ref[...]).astype(jnp.bfloat16)
            rotated_ref[some, at, :] = rotated.reshape(-1, block_rows, electrons)
        copy = pltpu.make_async_copy(
            rotated_ref.at[:, at], rotated_hbm.at[:, at], left.at[start // block_rows]
        )
        copy.start()
        outgoing.append(copy)
    for copy in outgoing:
        copy.wait()


def rotate(chol, trial):
    vectors, rows, _ = chol.shape
    blocks = rows // block_rows
    shape = (vectors, rows, trial.shape[1])
    return pl.pallas_call(
        rotate_kernel,
        in_specs=[IN_HBM, WHOLE],
        out_specs=IN_HBM,
        out_shape=jax.ShapeDtypeStruct(shape, jnp.bfloat16),
        scratch_shapes=[
            pltpu.VMEM(chol.shape, chol.dtype),
            pltpu.VMEM(shape, jnp.bfloat16),
            pltpu.SemaphoreType.DMA((2 * blocks,)),
            pltpu.SemaphoreType.DMA((blocks,)),
        ],
        compiler_params=params(50),
        cost_estimate=cost(2**32, 2**24),
    )(chol, trial)


def potential_kernel(mixed_ref, chol_hbm, out_ref, wide_ref, chol_ref, arrived):
    walkers, vectors = mixed_ref.shape
    _, rows, orbitals = chol_ref.shape
    incoming = fetch(chol_hbm, chol_ref, arrived)
    keep = diagonal(256 // block_rows)
    g = lax.broadcasted_iota(jnp.int32, (vectors, 256), 0)
    lane = lax.broadcasted_iota(jnp.int32, (vectors, 256), 1) // block_rows
    for start in range(0, vectors * block_rows, 256):
        pick = (g == start // block_rows + lane).astype(jnp.bfloat16)
        wide = jnp.where(keep, dot(mixed_ref[...], pick)[:, None, :], 0.0)
        wide_ref[:, start : start + 256] = wide.reshape(-1, 256).astype(jnp.bfloat16)
    for start in range(0, rows, block_rows):
        at = slice(start, start + block_rows)
        incoming[start, 0].wait()
        incoming[start, vectors // 2].wait()
        for low in range(0, orbitals, 256):
            right = chol_ref[:, at, low : low + 256].reshape(vectors * block_rows, 256)
            out = time_root * dot(wide_ref[...], right)
            out_ref[:, at, low : low + 256] = out.astype(jnp.bfloat16).reshape(walkers, block_rows, 256)


def potential(mixed, chol):
    walkers, vectors = mixed.shape
    _, rows, orbitals = chol.shape
    return pl.pallas_call(
        potential_kernel,
        in_specs=[WHOLE, IN_HBM],
        out_specs=WHOLE,
        out_shape=jax.ShapeDtypeStruct((walkers, rows, orbitals), jnp.bfloat16),
        scratch_shapes=[
            pltpu.VMEM((walkers * block_rows, vectors * block_rows), jnp.bfloat16),
            pltpu.VMEM(chol.shape, chol.dtype),
            pltpu.SemaphoreType.DMA((2 * rows // block_rows,)),
        ],
        compiler_params=params(50),
    )(mixed, chol)


def exchange(value, axis):
    return lax.all_to_all(value, axis, split_axis=0, concat_axis=0, tiled=True)


def swap(value, axis):
    return lax.ppermute(value, axis, [(0, 1), (1, 0)])


def spread(value, axis):
    count = lax.axis_size(axis)
    return exchange(jnp.broadcast_to(value[None], (count,) + value.shape), axis)


def turn(value, axis, shift):
    return lax.ppermute(value, axis, [(i, (i + shift) % 4) for i in range(4)])


def ring_sum(value, axis):
    return value + turn(value, axis, 1) + turn(value, axis, 2) + turn(value, axis, 3)


def row_sum(part, by_permutes):
    core = lax.axis_index("c")
    count = part.shape[0] // 2
    halves = part.reshape((2, count) + part.shape[1:])
    mine = lax.dynamic_index_in_dim(halves, core, 0, False)
    other = lax.dynamic_index_in_dim(halves, 1 - core, 0, False)
    total = mine + swap(other, "c")
    if by_permutes:
        total = ring_sum(ring_sum(total, "x"), "zh")
    else:
        total = jnp.sum(spread(total, ("x", "zh")), axis=0)
    other = swap(total, "c")
    return jnp.where(
        core == 0,
        jnp.concatenate([total, other]),
        jnp.concatenate([other, total]),
    )


def gather_trial(rows):
    core = lax.axis_index("c")
    mine = spread(rows, ("x", "zh"))
    other = swap(mine, "c")
    both = jnp.where(core == 0, jnp.stack([mine, other], 1), jnp.stack([other, mine], 1))
    return both.reshape(-1, rows.shape[-1])


def taylor(potential, walker):
    summed = walker.astype(jnp.float32)
    power_term = walker
    for degree in range(1, 5):
        next_term = jnp.dot(potential, power_term, preferred_element_type=jnp.float32) / degree
        summed = summed + next_term
        power_term = next_term.astype(jnp.bfloat16)
    return summed.astype(jnp.bfloat16)


def shards(cholesky, walkers, trial_orbitals, fields, log_weights):
    vectors, rows, orbitals = cholesky.shape
    walker_count, _, electrons = walkers.shape
    trial = gather_trial(trial_orbitals)
    phi = exchange(walkers, ROW).reshape(orbitals, electrons)
    part = first_bias(cholesky, trial, walkers)
    weights_now = log_weights
    steps = fields.shape[0]
    for step in range(steps):
        shifted = time_root * row_sum(part, by_permutes=step == 0)
        aux_field = fields[step]
        weights_now = weights_now + jnp.sum(aux_field * shifted - 0.5 * shifted * shifted, axis=1)
        mixed = (aux_field - shifted).astype(jnp.bfloat16)
        sent = potential(mixed, cholesky)
        if step == 0:
            sent, trial, phi = lax.optimization_barrier((sent, trial, phi))
            rotated = rotate(cholesky, trial)
        if step == steps - 1:
            paired = swap(weights_now, "zl")
            sent, paired = lax.optimization_barrier((sent, paired))
        sent = exchange(sent, ROW).reshape(orbitals, orbitals)
        if step == 0:
            sent, rotated = lax.optimization_barrier((sent, rotated))
        if step == steps - 1:
            paired = jnp.concatenate([weights_now, paired])
            everyone = [paired] + [turn(paired, "y", shift) for shift in range(1, 4)]
            weight_sum = jnp.sum(jnp.exp(jnp.concatenate(everyone)))
            count = walker_count * lax.axis_size(WALK)
            weights_now = weights_now - jnp.log(weight_sum / count)
        phi = taylor(sent, phi)
        if step == steps - 1:
            phi, weights_now = lax.optimization_barrier((phi, weights_now))
        phi_rows = exchange(phi.reshape(walker_count, rows, electrons), ROW)
        if step < steps - 1:
            part = bias(rotated, phi_rows)
    return phi_rows, weights_now


def solution(mesh):
    split = Mesh(mesh.devices.reshape(4, 4, 2, 4, 2), ROW + WALK)
    placed = (
        P(None, ROW, None),
        P(WALK, ROW, None),
        P(ROW, None),
        P(None, WALK, None),
        P(WALK),
    )
    return jax.shard_map(
        shards,
        mesh=split,
        in_specs=placed,
        out_specs=(P(WALK, ROW, None), P(WALK)),
        check_vma=False,
    )
```

```python
import functools

import jax
import jax.numpy as jnp
from jax import lax
from jax.experimental import pallas as pl
from jax.experimental.pallas import tpu as pltpu
from jax.sharding import Mesh, PartitionSpec as P

ROW = ("x", "zh", "c")
WALK = ("y", "zl")

block_rows = 8
time_root = 0.1
WHOLE = pl.BlockSpec(memory_space=pltpu.VMEM)
IN_HBM = pl.BlockSpec(memory_space=pltpu.HBM)
LAST = (((1,), (1,)), ((), ()))


def params(mebibytes):
    return pltpu.CompilerParams(vmem_limit_bytes=mebibytes * 2**20)


def cost(flops, size):
    return pl.CostEstimate(flops=flops, bytes_accessed=size, transcendentals=0)


def dot(left, right, dims=(((1,), (0,)), ((), ())), precision=None):
    return lax.dot_general(left, right, dims, precision=precision, preferred_element_type=jnp.float32)


def diagonal(walkers):
    shape = (1, block_rows, walkers * block_rows)
    lane = lax.broadcasted_iota(jnp.int32, shape, 2) % block_rows
    return lane == lax.broadcasted_iota(jnp.int32, shape, 1)


def reduce_diagonal(cross, walkers):
    kept = jnp.sum(jnp.where(diagonal(walkers), cross, 0.0), axis=1)
    shape = (walkers, walkers * block_rows)
    lane = lax.broadcasted_iota(jnp.int32, shape, 1) // block_rows
    pick = (lane == lax.broadcasted_iota(jnp.int32, shape, 0)).astype(jnp.float32)
    return dot(pick, kept, LAST, precision=lax.Precision.HIGHEST)


def diagonal(walkers):
    shape = (1, block_rows, walkers * block_rows)
    lane = lax.broadcasted_iota(jnp.int32, shape, 2) % block_rows
    return lane == lax.broadcasted_iota(jnp.int32, shape, 1)


def reduce_diagonal(cross, walkers):
    kept = jnp.sum(jnp.where(diagonal(walkers), cross, 0.0), axis=1)
    shape = (walkers, walkers * block_rows)
    lane = lax.broadcasted_iota(jnp.int32, shape, 1) // block_rows
    pick = (lane == lax.broadcasted_iota(jnp.int32, shape, 0)).astype(jnp.float32)
    return dot(pick, kept, LAST, precision=lax.Precision.HIGHEST)


def in_vmem(value):
    return pltpu.with_memory_space_constraint(value, pltpu.VMEM)


def pieces(vectors, rows):
    some = 512 // block_rows
    return [
        (slice(low, low + some), slice(start, start + block_rows))
        for low in range(0, vectors, some)
        for start in range(0, rows, block_rows)
    ]


def add_diagonal(rotated, phi_ref, at, some, cross_ref):
    right = phi_ref[:, at, :].reshape(-1, phi_ref.shape[2])
    cross = dot(rotated, right, LAST).reshape(-1, block_rows, right.shape[0])
    if at.start:
        cross = cross + cross_ref[some]
    cross_ref[some] = cross


def bias_kernel(rotated_ref, phi_ref, part_ref, cross_ref):
    vectors, rows, electrons = rotated_ref.shape
    for some, at in pieces(vectors, rows):
        add_diagonal(rotated_ref[some, at, :].reshape(-1, electrons), phi_ref, at, some, cross_ref)
    part_ref[...] = reduce_diagonal(cross_ref[...], phi_ref.shape[0])


def bias(rotated, phi):
    vectors = rotated.shape[0]
    walkers = phi.shape[0]
    return pl.pallas_call(
        bias_kernel,
        in_specs=[WHOLE] * 2,
        out_specs=WHOLE,
        out_shape=jax.ShapeDtypeStruct((walkers, vectors), jnp.float32),
        scratch_shapes=[pltpu.VMEM((vectors, block_rows, walkers * block_rows), jnp.float32)],
        compiler_params=params(12),
        cost_estimate=cost(2**30, 2**22),
    )(rotated, phi)


def fetch(chol_hbm, chol_ref, arrived):
    vectors, rows, _ = chol_ref.shape
    half = vectors // 2
    copies = {}
    for start in range(0, rows, block_rows):
        for low in range(0, vectors, half):
            at = (slice(low, low + half), slice(start, start + block_rows))
            copy = pltpu.make_async_copy(chol_hbm.at[at], chol_ref.at[at], arrived.at[len(copies)])
            copy.start()
            copies[start, low] = copy
    return copies


def first_bias_kernel(chol_hbm, trial_ref, phi_ref, part_ref, chol_ref, paired_ref, cross_ref, arrived):
    vectors, rows, orbitals = chol_ref.shape
    incoming = fetch(chol_hbm, chol_ref, arrived)
    for start in range(0, rows, block_rows):
        phi = phi_ref[:, start : start + block_rows, :].reshape(-1, phi_ref.shape[2])
        paired_ref[start // block_rows] = dot(phi, trial_ref[...], LAST).astype(jnp.bfloat16)
    some = 512 // block_rows
    for start in range(0, rows, block_rows):
        for low in range(0, vectors, some):
            if (start, low) in incoming:
                incoming[start, low].wait()
            piece = chol_ref[low : low + some, start : start + block_rows, :].reshape(-1, orbitals)
            cross = dot(piece, paired_ref[start // block_rows], LAST).reshape(some, block_rows, -1)
            if start:
                cross = cross + cross_ref[low : low + some]
            cross_ref[low : low + some] = cross
    part_ref[...] = reduce_diagonal(cross_ref[...], phi_ref.shape[0])


def first_bias(chol, trial, phi):
    vectors, rows, orbitals = chol.shape
    walkers = phi.shape[0]
    blocks = rows // block_rows
    wide = walkers * block_rows
    return pl.pallas_call(
        first_bias_kernel,
        in_specs=[IN_HBM, WHOLE, WHOLE],
        out_specs=WHOLE,
        out_shape=jax.ShapeDtypeStruct((walkers, vectors), jnp.float32),
        scratch_shapes=[
            pltpu.VMEM(chol.shape, chol.dtype),
            pltpu.VMEM((blocks, wide, orbitals), jnp.bfloat16),
            pltpu.VMEM((vectors, block_rows, wide), jnp.float32),
            pltpu.SemaphoreType.DMA((2 * blocks,)),
        ],
        compiler_params=params(50),
        cost_estimate=cost(2**32, 2**24),
    )(chol, trial, phi)


def rotate_kernel(chol_hbm, trial_ref, rotated_hbm, chol_ref, rotated_ref, arrived, left):
    vectors, rows, orbitals = chol_ref.shape
    electrons = trial_ref.shape[1]
    incoming = fetch(chol_hbm, chol_ref, arrived)
    outgoing = []
    for start in range(0, rows, block_rows):
        at = slice(start, start + block_rows)
        for low in range(0, vectors, 512 // block_rows):
            if (start, low) in incoming:
                incoming[start, low].wait()
            some = slice(low, low + 512 // block_rows)
            piece = chol_ref[some, at, :].reshape(-1, orbitals)
            rotated = dot(piece, trial_ref[...]).astype(jnp.bfloat16)
            rotated_ref[some, at, :] = rotated.reshape(-1, block_rows, electrons)
        copy = pltpu.make_async_copy(
            rotated_ref.at[:, at], rotated_hbm.at[:, at], left.at[start // block_rows]
        )
        copy.start()
        outgoing.append(copy)
    for copy in outgoing:
        copy.wait()


def rotate(chol, trial):
    vectors, rows, _ = chol.shape
    blocks = rows // block_rows
    shape = (vectors, rows, trial.shape[1])
    return pl.pallas_call(
        rotate_kernel,
        in_specs=[IN_HBM, WHOLE],
        out_specs=IN_HBM,
        out_shape=jax.ShapeDtypeStruct(shape, jnp.bfloat16),
        scratch_shapes=[
            pltpu.VMEM(chol.shape, chol.dtype),
            pltpu.VMEM(shape, jnp.bfloat16),
            pltpu.SemaphoreType.DMA((2 * blocks,)),
            pltpu.SemaphoreType.DMA((blocks,)),
        ],
        compiler_params=params(50),
        cost_estimate=cost(2**32, 2**24),
    )(chol, trial)


def potential_kernel(mixed_ref, chol_hbm, out_ref, wide_ref, chol_ref, arrived):
    walkers, vectors = mixed_ref.shape
    _, rows, orbitals = chol_ref.shape
    incoming = fetch(chol_hbm, chol_ref, arrived)
    keep = diagonal(256 // block_rows)
    g = lax.broadcasted_iota(jnp.int32, (vectors, 256), 0)
    lane = lax.broadcasted_iota(jnp.int32, (vectors, 256), 1) // block_rows
    for start in range(0, vectors * block_rows, 256):
        pick = (g == start // block_rows + lane).astype(jnp.bfloat16)
        wide = jnp.where(keep, dot(mixed_ref[...], pick)[:, None, :], 0.0)
        wide_ref[:, start : start + 256] = wide.reshape(-1, 256).astype(jnp.bfloat16)
    for start in range(0, rows, block_rows):
        at = slice(start, start + block_rows)
        incoming[start, 0].wait()
        incoming[start, vectors // 2].wait()
        for low in range(0, orbitals, 256):
            right = chol_ref[:, at, low : low + 256].reshape(vectors * block_rows, 256)
            out = time_root * dot(wide_ref[...], right)
            out_ref[:, at, low : low + 256] = out.astype(jnp.bfloat16).reshape(walkers, block_rows, 256)


def potential(mixed, chol):
    walkers, vectors = mixed.shape
    _, rows, orbitals = chol.shape
    return pl.pallas_call(
        potential_kernel,
        in_specs=[WHOLE, IN_HBM],
        out_specs=WHOLE,
        out_shape=jax.ShapeDtypeStruct((walkers, rows, orbitals), jnp.bfloat16),
        scratch_shapes=[
            pltpu.VMEM((walkers * block_rows, vectors * block_rows), jnp.bfloat16),
            pltpu.VMEM(chol.shape, chol.dtype),
            pltpu.SemaphoreType.DMA((2 * rows // block_rows,)),
        ],
        compiler_params=params(50),
    )(mixed, chol)


def exchange(value, axis):
    return lax.all_to_all(value, axis, split_axis=0, concat_axis=0, tiled=True)


def swap(value, axis):
    return lax.ppermute(value, axis, [(0, 1), (1, 0)])


def spread(value, axis):
    count = lax.axis_size(axis)
    return exchange(jnp.broadcast_to(value[None], (count,) + value.shape), axis)


def turn(value, axis, shift):
    return lax.ppermute(value, axis, [(i, (i + shift) % 4) for i in range(4)])


def ring_sum(value, axis):
    return value + turn(value, axis, 1) + turn(value, axis, 2) + turn(value, axis, 3)


def row_sum(part, by_permutes):
    core = lax.axis_index("c")
    count = part.shape[0] // 2
    halves = part.reshape((2, count) + part.shape[1:])
    mine = lax.dynamic_index_in_dim(halves, core, 0, False)
    other = lax.dynamic_index_in_dim(halves, 1 - core, 0, False)
    total = mine + swap(other, "c")
    if by_permutes:
        total = ring_sum(ring_sum(total, "x"), "zh")
    else:
        total = jnp.sum(spread(total, ("x", "zh")), axis=0)
    other = swap(total, "c")
    return jnp.where(
        core == 0,
        jnp.concatenate([total, other]),
        jnp.concatenate([other, total]),
    )


def gather_trial(rows):
    core = lax.axis_index("c")
    mine = spread(rows, ("x", "zh"))
    other = swap(mine, "c")
    both = jnp.where(core == 0, jnp.stack([mine, other], 1), jnp.stack([other, mine], 1))
    return both.reshape(-1, rows.shape[-1])


def taylor(potential, walker):
    summed = walker.astype(jnp.float32)
    power_term = walker
    for degree in range(1, 5):
        next_term = jnp.dot(potential, power_term, preferred_element_type=jnp.float32) / degree
        summed = summed + next_term
        power_term = next_term.astype(jnp.bfloat16)
    return summed.astype(jnp.bfloat16)


def shards(cholesky, walkers, trial_orbitals, fields, log_weights):
    vectors, rows, orbitals = cholesky.shape
    walker_count, _, electrons = walkers.shape
    trial = gather_trial(trial_orbitals)
    phi = exchange(walkers, ROW).reshape(orbitals, electrons)
    part = first_bias(cholesky, trial, walkers)
    weights_now = log_weights
    steps = fields.shape[0]
    for step in range(steps):
        shifted = time_root * row_sum(part, by_permutes=step == 0)
        aux_field = fields[step]
        weights_now = weights_now + jnp.sum(aux_field * shifted - 0.5 * shifted * shifted, axis=1)
        mixed = (aux_field - shifted).astype(jnp.bfloat16)
        sent = potential(mixed, cholesky)
        if step == 0:
            sent, trial, phi = lax.optimization_barrier((sent, trial, phi))
            rotated = rotate(cholesky, trial)
        if step == steps - 1:
            paired = swap(weights_now, "zl")
            sent, paired = lax.optimization_barrier((sent, paired))
        sent = exchange(sent, ROW).reshape(orbitals, orbitals)
        if step == 0:
            sent, rotated = lax.optimization_barrier((sent, rotated))
        phi = taylor(sent, phi)
        if step == steps - 1:
            phi, paired = lax.optimization_barrier((phi, paired))
            paired = jnp.concatenate([weights_now, paired])
            everyone = [paired] + [turn(paired, "y", shift) for shift in range(1, 4)]
            weight_sum = jnp.sum(jnp.exp(jnp.concatenate(everyone)))
            count = walker_count * lax.axis_size(WALK)
            weights_now = weights_now - jnp.log(weight_sum / count)
        phi_rows = exchange(phi.reshape(walker_count, rows, electrons), ROW)
        if step < steps - 1:
            part = bias(rotated, phi_rows)
    return phi_rows, weights_now


def solution(mesh):
    split = Mesh(mesh.devices.reshape(4, 4, 2, 4, 2), ROW + WALK)
    placed = (
        P(None, ROW, None),
        P(WALK, ROW, None),
        P(ROW, None),
        P(None, WALK, None),
        P(WALK),
    )
    return jax.shard_map(
        shards,
        mesh=split,
        in_specs=placed,
        out_specs=(P(WALK, ROW, None), P(WALK)),
        check_vma=False,
    )
```

```python
import functools

import jax
import jax.numpy as jnp
from jax import lax
from jax.experimental import pallas as pl
from jax.experimental.pallas import tpu as pltpu
from jax.sharding import Mesh, PartitionSpec as P

ROW = ("x", "zh", "c")
WALK = ("y", "zl")

block_rows = 8
time_root = 0.1
WHOLE = pl.BlockSpec(memory_space=pltpu.VMEM)
IN_HBM = pl.BlockSpec(memory_space=pltpu.HBM)
LAST = (((1,), (1,)), ((), ()))


def params(mebibytes):
    return pltpu.CompilerParams(vmem_limit_bytes=mebibytes * 2**20)


def cost(flops, size):
    return pl.CostEstimate(flops=flops, bytes_accessed=size, transcendentals=0)


def dot(left, right, dims=(((1,), (0,)), ((), ())), precision=None):
    return lax.dot_general(left, right, dims, precision=precision, preferred_element_type=jnp.float32)


def diagonal(walkers):
    shape = (1, block_rows, walkers * block_rows)
    lane = lax.broadcasted_iota(jnp.int32, shape, 2) % block_rows
    return lane == lax.broadcasted_iota(jnp.int32, shape, 1)


def reduce_diagonal(cross, walkers):
    kept = jnp.sum(jnp.where(diagonal(walkers), cross, 0.0), axis=1)
    shape = (walkers, walkers * block_rows)
    lane = lax.broadcasted_iota(jnp.int32, shape, 1) // block_rows
    pick = (lane == lax.broadcasted_iota(jnp.int32, shape, 0)).astype(jnp.float32)
    return dot(pick, kept, LAST, precision=lax.Precision.HIGHEST)


def diagonal(walkers):
    shape = (1, block_rows, walkers * block_rows)
    lane = lax.broadcasted_iota(jnp.int32, shape, 2) % block_rows
    return lane == lax.broadcasted_iota(jnp.int32, shape, 1)


def reduce_diagonal(cross, walkers):
    kept = jnp.sum(jnp.where(diagonal(walkers), cross, 0.0), axis=1)
    shape = (walkers, walkers * block_rows)
    lane = lax.broadcasted_iota(jnp.int32, shape, 1) // block_rows
    pick = (lane == lax.broadcasted_iota(jnp.int32, shape, 0)).astype(jnp.float32)
    return dot(pick, kept, LAST, precision=lax.Precision.HIGHEST)


def in_vmem(value):
    return pltpu.with_memory_space_constraint(value, pltpu.VMEM)


def pieces(vectors, rows):
    some = 512 // block_rows
    return [
        (slice(low, low + some), slice(start, start + block_rows))
        for low in range(0, vectors, some)
        for start in range(0, rows, block_rows)
    ]


def add_diagonal(rotated, phi_ref, at, some, cross_ref):
    right = phi_ref[:, at, :].reshape(-1, phi_ref.shape[2])
    cross = dot(rotated, right, LAST).reshape(-1, block_rows, right.shape[0])
    if at.start:
        cross = cross + cross_ref[some]
    cross_ref[some] = cross


def bias_kernel(rotated_ref, phi_ref, part_ref, cross_ref):
    vectors, rows, electrons = rotated_ref.shape
    for some, at in pieces(vectors, rows):
        add_diagonal(rotated_ref[some, at, :].reshape(-1, electrons), phi_ref, at, some, cross_ref)
    part_ref[...] = reduce_diagonal(cross_ref[...], phi_ref.shape[0])


def bias(rotated, phi):
    vectors = rotated.shape[0]
    walkers = phi.shape[0]
    return pl.pallas_call(
        bias_kernel,
        in_specs=[WHOLE] * 2,
        out_specs=WHOLE,
        out_shape=jax.ShapeDtypeStruct((walkers, vectors), jnp.float32),
        scratch_shapes=[pltpu.VMEM((vectors, block_rows, walkers * block_rows), jnp.float32)],
        compiler_params=params(12),
        cost_estimate=cost(2**30, 2**22),
    )(rotated, phi)


def fetch(chol_hbm, chol_ref, arrived):
    vectors, rows, _ = chol_ref.shape
    half = vectors // 2
    copies = {}
    for start in range(0, rows, block_rows):
        for low in range(0, vectors, half):
            at = (slice(low, low + half), slice(start, start + block_rows))
            copy = pltpu.make_async_copy(chol_hbm.at[at], chol_ref.at[at], arrived.at[len(copies)])
            copy.start()
            copies[start, low] = copy
    return copies


def first_bias_kernel(chol_hbm, trial_ref, phi_ref, part_ref, chol_ref, paired_ref, cross_ref, arrived):
    vectors, rows, orbitals = chol_ref.shape
    incoming = fetch(chol_hbm, chol_ref, arrived)
    for start in range(0, rows, block_rows):
        phi = phi_ref[:, start : start + block_rows, :].reshape(-1, phi_ref.shape[2])
        paired_ref[start // block_rows] = dot(phi, trial_ref[...], LAST).astype(jnp.bfloat16)
    some = 512 // block_rows
    for start in range(0, rows, block_rows):
        for low in range(0, vectors, some):
            if (start, low) in incoming:
                incoming[start, low].wait()
            piece = chol_ref[low : low + some, start : start + block_rows, :].reshape(-1, orbitals)
            cross = dot(piece, paired_ref[start // block_rows], LAST).reshape(some, block_rows, -1)
            if start:
                cross = cross + cross_ref[low : low + some]
            cross_ref[low : low + some] = cross
    part_ref[...] = reduce_diagonal(cross_ref[...], phi_ref.shape[0])


def first_bias(chol, trial, phi):
    vectors, rows, orbitals = chol.shape
    walkers = phi.shape[0]
    blocks = rows // block_rows
    wide = walkers * block_rows
    return pl.pallas_call(
        first_bias_kernel,
        in_specs=[IN_HBM, WHOLE, WHOLE],
        out_specs=WHOLE,
        out_shape=jax.ShapeDtypeStruct((walkers, vectors), jnp.float32),
        scratch_shapes=[
            pltpu.VMEM(chol.shape, chol.dtype),
            pltpu.VMEM((blocks, wide, orbitals), jnp.bfloat16),
            pltpu.VMEM((vectors, block_rows, wide), jnp.float32),
            pltpu.SemaphoreType.DMA((2 * blocks,)),
        ],
        compiler_params=params(50),
        cost_estimate=cost(2**32, 2**24),
    )(chol, trial, phi)


def rotate_kernel(chol_hbm, trial_ref, rotated_hbm, chol_ref, rotated_ref, arrived, left):
    vectors, rows, orbitals = chol_ref.shape
    electrons = trial_ref.shape[1]
    incoming = fetch(chol_hbm, chol_ref, arrived)
    outgoing = []
    for start in range(0, rows, block_rows):
        at = slice(start, start + block_rows)
        for low in range(0, vectors, 512 // block_rows):
            if (start, low) in incoming:
                incoming[start, low].wait()
            some = slice(low, low + 512 // block_rows)
            piece = chol_ref[some, at, :].reshape(-1, orbitals)
            rotated = dot(piece, trial_ref[...]).astype(jnp.bfloat16)
            rotated_ref[some, at, :] = rotated.reshape(-1, block_rows, electrons)
        copy = pltpu.make_async_copy(
            rotated_ref.at[:, at], rotated_hbm.at[:, at], left.at[start // block_rows]
        )
        copy.start()
        outgoing.append(copy)
    for copy in outgoing:
        copy.wait()


def rotate(chol, trial):
    vectors, rows, _ = chol.shape
    blocks = rows // block_rows
    shape = (vectors, rows, trial.shape[1])
    return pl.pallas_call(
        rotate_kernel,
        in_specs=[IN_HBM, WHOLE],
        out_specs=IN_HBM,
        out_shape=jax.ShapeDtypeStruct(shape, jnp.bfloat16),
        scratch_shapes=[
            pltpu.VMEM(chol.shape, chol.dtype),
            pltpu.VMEM(shape, jnp.bfloat16),
            pltpu.SemaphoreType.DMA((2 * blocks,)),
            pltpu.SemaphoreType.DMA((blocks,)),
        ],
        compiler_params=params(50),
        cost_estimate=cost(2**32, 2**24),
    )(chol, trial)


def potential_kernel(mixed_ref, chol_hbm, out_ref, wide_ref, chol_ref, arrived):
    walkers, vectors = mixed_ref.shape
    _, rows, orbitals = chol_ref.shape
    incoming = fetch(chol_hbm, chol_ref, arrived)
    keep = diagonal(256 // block_rows)
    g = lax.broadcasted_iota(jnp.int32, (vectors, 256), 0)
    lane = lax.broadcasted_iota(jnp.int32, (vectors, 256), 1) // block_rows
    for start in range(0, vectors * block_rows, 256):
        pick = (g == start // block_rows + lane).astype(jnp.bfloat16)
        wide = jnp.where(keep, dot(mixed_ref[...], pick)[:, None, :], 0.0)
        wide_ref[:, start : start + 256] = wide.reshape(-1, 256).astype(jnp.bfloat16)
    for start in range(0, rows, block_rows):
        at = slice(start, start + block_rows)
        incoming[start, 0].wait()
        incoming[start, vectors // 2].wait()
        for low in range(0, orbitals, 256):
            right = chol_ref[:, at, low : low + 256].reshape(vectors * block_rows, 256)
            out = time_root * dot(wide_ref[...], right)
            out_ref[:, at, low : low + 256] = out.astype(jnp.bfloat16).reshape(walkers, block_rows, 256)


def potential(mixed, chol):
    walkers, vectors = mixed.shape
    _, rows, orbitals = chol.shape
    return pl.pallas_call(
        potential_kernel,
        in_specs=[WHOLE, IN_HBM],
        out_specs=WHOLE,
        out_shape=jax.ShapeDtypeStruct((walkers, rows, orbitals), jnp.bfloat16),
        scratch_shapes=[
            pltpu.VMEM((walkers * block_rows, vectors * block_rows), jnp.bfloat16),
            pltpu.VMEM(chol.shape, chol.dtype),
            pltpu.SemaphoreType.DMA((2 * rows // block_rows,)),
        ],
        compiler_params=params(50),
    )(mixed, chol)


def exchange(value, axis):
    return lax.all_to_all(value, axis, split_axis=0, concat_axis=0, tiled=True)


def swap(value, axis):
    return lax.ppermute(value, axis, [(0, 1), (1, 0)])


def spread(value, axis):
    count = lax.axis_size(axis)
    return exchange(jnp.broadcast_to(value[None], (count,) + value.shape), axis)


def turn(value, axis, shift):
    return lax.ppermute(value, axis, [(i, (i + shift) % 4) for i in range(4)])


def ring_sum(value, axis):
    return value + turn(value, axis, 1) + turn(value, axis, 2) + turn(value, axis, 3)


def row_sum(part, by_permutes):
    core = lax.axis_index("c")
    count = part.shape[0] // 2
    halves = part.reshape((2, count) + part.shape[1:])
    mine = lax.dynamic_index_in_dim(halves, core, 0, False)
    other = lax.dynamic_index_in_dim(halves, 1 - core, 0, False)
    total = mine + swap(other, "c")
    if by_permutes:
        total = ring_sum(ring_sum(total, "x"), "zh")
    else:
        total = jnp.sum(spread(total, ("x", "zh")), axis=0)
    other = swap(total, "c")
    return jnp.where(
        core == 0,
        jnp.concatenate([total, other]),
        jnp.concatenate([other, total]),
    )


def gather_trial(rows):
    core = lax.axis_index("c")
    mine = spread(rows, ("x", "zh"))
    other = swap(mine, "c")
    both = jnp.where(core == 0, jnp.stack([mine, other], 1), jnp.stack([other, mine], 1))
    return both.reshape(-1, rows.shape[-1])


def taylor_kernel(potential_ref, walker_ref, out_ref, term_ref, summed_ref):
    orbitals = potential_ref.shape[0]
    count = 512
    for degree in range(1, 5):
        held = walker_ref if degree == 1 else term_ref.at[degree % 2]
        for low in range(0, orbitals, count):
            at = slice(low, low + count)
            next_term = dot(potential_ref[at, :], held[...]) / degree
            before = walker_ref[at, :].astype(jnp.float32) if degree == 1 else summed_ref[at, :]
            if degree < 4:
                summed_ref[at, :] = before + next_term
                term_ref[(degree + 1) % 2, at, :] = next_term.astype(jnp.bfloat16)
            else:
                out_ref[at, :] = (before + next_term).astype(jnp.bfloat16)


def taylor(potential, walker):
    return pl.pallas_call(
        taylor_kernel,
        in_specs=[WHOLE] * 2,
        out_specs=WHOLE,
        out_shape=jax.ShapeDtypeStruct(walker.shape, jnp.bfloat16),
        scratch_shapes=[
            pltpu.VMEM((2,) + walker.shape, jnp.bfloat16),
            pltpu.VMEM(walker.shape, jnp.float32),
        ],
        compiler_params=params(12),
        cost_estimate=cost(2**31, 2**22),
    )(potential, walker)


def shards(cholesky, walkers, trial_orbitals, fields, log_weights):
    vectors, rows, orbitals = cholesky.shape
    walker_count, _, electrons = walkers.shape
    trial = gather_trial(trial_orbitals)
    phi = exchange(walkers, ROW).reshape(orbitals, electrons)
    part = first_bias(cholesky, trial, walkers)
    weights_now = log_weights
    steps = fields.shape[0]
    for step in range(steps):
        shifted = time_root * row_sum(part, by_permutes=step == 0)
        aux_field = fields[step]
        weights_now = weights_now + jnp.sum(aux_field * shifted - 0.5 * shifted * shifted, axis=1)
        mixed = (aux_field - shifted).astype(jnp.bfloat16)
        sent = potential(mixed, cholesky)
        if step == 0:
            sent, trial, phi = lax.optimization_barrier((sent, trial, phi))
            rotated = rotate(cholesky, trial)
        if step == steps - 1:
            paired = swap(weights_now, "zl")
            sent, paired = lax.optimization_barrier((sent, paired))
        sent = exchange(sent, ROW).reshape(orbitals, orbitals)
        if step == 0:
            sent, rotated = lax.optimization_barrier((sent, rotated))
        phi = taylor(sent, phi)
        if step == steps - 1:
            phi, paired = lax.optimization_barrier((phi, paired))
            paired = jnp.concatenate([weights_now, paired])
            everyone = [paired] + [turn(paired, "y", shift) for shift in range(1, 4)]
            weight_sum = jnp.sum(jnp.exp(jnp.concatenate(everyone)))
            count = walker_count * lax.axis_size(WALK)
            weights_now = weights_now - jnp.log(weight_sum / count)
        phi_rows = exchange(phi.reshape(walker_count, rows, electrons), ROW)
        if step < steps - 1:
            part = bias(rotated, phi_rows)
    return phi_rows, weights_now


def solution(mesh):
    split = Mesh(mesh.devices.reshape(4, 4, 2, 4, 2), ROW + WALK)
    placed = (
        P(None, ROW, None),
        P(WALK, ROW, None),
        P(ROW, None),
        P(None, WALK, None),
        P(WALK),
    )
    return jax.shard_map(
        shards,
        mesh=split,
        in_specs=placed,
        out_specs=(P(WALK, ROW, None), P(WALK)),
        check_vma=False,
    )
```

```python
import functools

import jax
import jax.numpy as jnp
from jax import lax
from jax.experimental import pallas as pl
from jax.experimental.pallas import tpu as pltpu
from jax.sharding import Mesh, PartitionSpec as P

ROW = ("x", "zh", "c")
WALK = ("y", "zl")

block_rows = 8
time_root = 0.1
WHOLE = pl.BlockSpec(memory_space=pltpu.VMEM)
IN_HBM = pl.BlockSpec(memory_space=pltpu.HBM)
LAST = (((1,), (1,)), ((), ()))


def params(mebibytes):
    return pltpu.CompilerParams(vmem_limit_bytes=mebibytes * 2**20)


def cost(flops, size):
    return pl.CostEstimate(flops=flops, bytes_accessed=size, transcendentals=0)


def dot(left, right, dims=(((1,), (0,)), ((), ())), precision=None):
    return lax.dot_general(left, right, dims, precision=precision, preferred_element_type=jnp.float32)


def diagonal(walkers):
    shape = (1, block_rows, walkers * block_rows)
    lane = lax.broadcasted_iota(jnp.int32, shape, 2) % block_rows
    return lane == lax.broadcasted_iota(jnp.int32, shape, 1)


def reduce_diagonal(cross, walkers):
    kept = jnp.sum(jnp.where(diagonal(walkers), cross, 0.0), axis=1)
    shape = (walkers, walkers * block_rows)
    lane = lax.broadcasted_iota(jnp.int32, shape, 1) // block_rows
    pick = (lane == lax.broadcasted_iota(jnp.int32, shape, 0)).astype(jnp.float32)
    return dot(pick, kept, LAST, precision=lax.Precision.HIGHEST)


def diagonal(walkers):
    shape = (1, block_rows, walkers * block_rows)
    lane = lax.broadcasted_iota(jnp.int32, shape, 2) % block_rows
    return lane == lax.broadcasted_iota(jnp.int32, shape, 1)


def reduce_diagonal(cross, walkers):
    kept = jnp.sum(jnp.where(diagonal(walkers), cross, 0.0), axis=1)
    shape = (walkers, walkers * block_rows)
    lane = lax.broadcasted_iota(jnp.int32, shape, 1) // block_rows
    pick = (lane == lax.broadcasted_iota(jnp.int32, shape, 0)).astype(jnp.float32)
    return dot(pick, kept, LAST, precision=lax.Precision.HIGHEST)


def in_vmem(value):
    return pltpu.with_memory_space_constraint(value, pltpu.VMEM)


def pieces(vectors, rows):
    some = 512 // block_rows
    return [
        (slice(low, low + some), slice(start, start + block_rows))
        for low in range(0, vectors, some)
        for start in range(0, rows, block_rows)
    ]


def add_diagonal(rotated, phi_ref, at, some, cross_ref):
    right = phi_ref[:, at, :].reshape(-1, phi_ref.shape[2])
    cross = dot(rotated, right, LAST).reshape(-1, block_rows, right.shape[0])
    if at.start:
        cross = cross + cross_ref[some]
    cross_ref[some] = cross


def bias_kernel(rotated_ref, phi_ref, part_ref, cross_ref):
    vectors, rows, electrons = rotated_ref.shape
    for some, at in pieces(vectors, rows):
        add_diagonal(rotated_ref[some, at, :].reshape(-1, electrons), phi_ref, at, some, cross_ref)
    part_ref[...] = reduce_diagonal(cross_ref[...], phi_ref.shape[0])


def bias(rotated, phi):
    vectors = rotated.shape[0]
    walkers = phi.shape[0]
    return pl.pallas_call(
        bias_kernel,
        in_specs=[WHOLE] * 2,
        out_specs=WHOLE,
        out_shape=jax.ShapeDtypeStruct((walkers, vectors), jnp.float32),
        scratch_shapes=[pltpu.VMEM((vectors, block_rows, walkers * block_rows), jnp.float32)],
        compiler_params=params(12),
        cost_estimate=cost(2**30, 2**22),
    )(rotated, phi)


def fetch(chol_hbm, chol_ref, arrived):
    vectors, rows, _ = chol_ref.shape
    half = vectors // 2
    copies = {}
    for start in range(0, rows, block_rows):
        for low in range(0, vectors, half):
            at = (slice(low, low + half), slice(start, start + block_rows))
            copy = pltpu.make_async_copy(chol_hbm.at[at], chol_ref.at[at], arrived.at[len(copies)])
            copy.start()
            copies[start, low] = copy
    return copies


def first_bias_kernel(chol_hbm, trial_ref, phi_ref, part_ref, chol_ref, paired_ref, cross_ref, arrived):
    vectors, rows, orbitals = chol_ref.shape
    incoming = fetch(chol_hbm, chol_ref, arrived)
    for start in range(0, rows, block_rows):
        phi = phi_ref[:, start : start + block_rows, :].reshape(-1, phi_ref.shape[2])
        paired_ref[start // block_rows] = dot(phi, trial_ref[...], LAST).astype(jnp.bfloat16)
    some = 512 // block_rows
    for start in range(0, rows, block_rows):
        for low in range(0, vectors, some):
            if (start, low) in incoming:
                incoming[start, low].wait()
            piece = chol_ref[low : low + some, start : start + block_rows, :].reshape(-1, orbitals)
            cross = dot(piece, paired_ref[start // block_rows], LAST).reshape(some, block_rows, -1)
            if start:
                cross = cross + cross_ref[low : low + some]
            cross_ref[low : low + some] = cross
    part_ref[...] = reduce_diagonal(cross_ref[...], phi_ref.shape[0])


def first_bias(chol, trial, phi):
    vectors, rows, orbitals = chol.shape
    walkers = phi.shape[0]
    blocks = rows // block_rows
    wide = walkers * block_rows
    return pl.pallas_call(
        first_bias_kernel,
        in_specs=[IN_HBM, WHOLE, WHOLE],
        out_specs=WHOLE,
        out_shape=jax.ShapeDtypeStruct((walkers, vectors), jnp.float32),
        scratch_shapes=[
            pltpu.VMEM(chol.shape, chol.dtype),
            pltpu.VMEM((blocks, wide, orbitals), jnp.bfloat16),
            pltpu.VMEM((vectors, block_rows, wide), jnp.float32),
            pltpu.SemaphoreType.DMA((2 * blocks,)),
        ],
        compiler_params=params(50),
        cost_estimate=cost(2**32, 2**24),
    )(chol, trial, phi)


def rotate_kernel(chol_hbm, trial_ref, rotated_hbm, chol_ref, rotated_ref, arrived, left):
    vectors, rows, orbitals = chol_ref.shape
    electrons = trial_ref.shape[1]
    incoming = fetch(chol_hbm, chol_ref, arrived)
    outgoing = []
    for start in range(0, rows, block_rows):
        at = slice(start, start + block_rows)
        for low in range(0, vectors, 512 // block_rows):
            if (start, low) in incoming:
                incoming[start, low].wait()
            some = slice(low, low + 512 // block_rows)
            piece = chol_ref[some, at, :].reshape(-1, orbitals)
            rotated = dot(piece, trial_ref[...]).astype(jnp.bfloat16)
            rotated_ref[some, at, :] = rotated.reshape(-1, block_rows, electrons)
        copy = pltpu.make_async_copy(
            rotated_ref.at[:, at], rotated_hbm.at[:, at], left.at[start // block_rows]
        )
        copy.start()
        outgoing.append(copy)
    for copy in outgoing:
        copy.wait()


def rotate(chol, trial):
    vectors, rows, _ = chol.shape
    blocks = rows // block_rows
    shape = (vectors, rows, trial.shape[1])
    return pl.pallas_call(
        rotate_kernel,
        in_specs=[IN_HBM, WHOLE],
        out_specs=IN_HBM,
        out_shape=jax.ShapeDtypeStruct(shape, jnp.bfloat16),
        scratch_shapes=[
            pltpu.VMEM(chol.shape, chol.dtype),
            pltpu.VMEM(shape, jnp.bfloat16),
            pltpu.SemaphoreType.DMA((2 * blocks,)),
            pltpu.SemaphoreType.DMA((blocks,)),
        ],
        compiler_params=params(50),
        cost_estimate=cost(2**32, 2**24),
    )(chol, trial)


def potential_kernel(mixed_ref, chol_hbm, out_ref, wide_ref, chol_ref, arrived):
    walkers, vectors = mixed_ref.shape
    _, rows, orbitals = chol_ref.shape
    incoming = fetch(chol_hbm, chol_ref, arrived)
    keep = diagonal(256 // block_rows)
    g = lax.broadcasted_iota(jnp.int32, (vectors, 256), 0)
    lane = lax.broadcasted_iota(jnp.int32, (vectors, 256), 1) // block_rows
    for start in range(0, vectors * block_rows, 256):
        pick = (g == start // block_rows + lane).astype(jnp.bfloat16)
        wide = jnp.where(keep, dot(mixed_ref[...], pick)[:, None, :], 0.0)
        wide_ref[:, start : start + 256] = wide.reshape(-1, 256).astype(jnp.bfloat16)
    for start in range(0, rows, block_rows):
        at = slice(start, start + block_rows)
        incoming[start, 0].wait()
        incoming[start, vectors // 2].wait()
        for low in range(0, orbitals, 256):
            right = chol_ref[:, at, low : low + 256].reshape(vectors * block_rows, 256)
            out = time_root * dot(wide_ref[...], right)
            out_ref[:, at, low : low + 256] = out.astype(jnp.bfloat16).reshape(walkers, block_rows, 256)


def potential(mixed, chol):
    walkers, vectors = mixed.shape
    _, rows, orbitals = chol.shape
    return pl.pallas_call(
        potential_kernel,
        in_specs=[WHOLE, IN_HBM],
        out_specs=WHOLE,
        out_shape=jax.ShapeDtypeStruct((walkers, rows, orbitals), jnp.bfloat16),
        scratch_shapes=[
            pltpu.VMEM((walkers * block_rows, vectors * block_rows), jnp.bfloat16),
            pltpu.VMEM(chol.shape, chol.dtype),
            pltpu.SemaphoreType.DMA((2 * rows // block_rows,)),
        ],
        compiler_params=params(50),
    )(mixed, chol)


def exchange(value, axis):
    return lax.all_to_all(value, axis, split_axis=0, concat_axis=0, tiled=True)


def swap(value, axis):
    return lax.ppermute(value, axis, [(0, 1), (1, 0)])


def spread(value, axis):
    count = lax.axis_size(axis)
    return exchange(jnp.broadcast_to(value[None], (count,) + value.shape), axis)


def turn(value, axis, shift):
    return lax.ppermute(value, axis, [(i, (i + shift) % 4) for i in range(4)])


def ring_sum(value, axis):
    return value + turn(value, axis, 1) + turn(value, axis, 2) + turn(value, axis, 3)


def row_sum(part, by_permutes):
    core = lax.axis_index("c")
    count = part.shape[0] // 2
    halves = part.reshape((2, count) + part.shape[1:])
    mine = lax.dynamic_index_in_dim(halves, core, 0, False)
    other = lax.dynamic_index_in_dim(halves, 1 - core, 0, False)
    total = mine + swap(other, "c")
    if by_permutes:
        total = ring_sum(ring_sum(total, "x"), "zh")
    else:
        total = jnp.sum(spread(total, ("x", "zh")), axis=0)
    other = swap(total, "c")
    return jnp.where(
        core == 0,
        jnp.concatenate([total, other]),
        jnp.concatenate([other, total]),
    )


def gather_trial(rows):
    core = lax.axis_index("c")
    mine = spread(rows, ("x", "zh"))
    other = swap(mine, "c")
    both = jnp.where(core == 0, jnp.stack([mine, other], 1), jnp.stack([other, mine], 1))
    return both.reshape(-1, rows.shape[-1])


def taylor_kernel(potential_ref, walker_ref, out_ref, term_ref, summed_ref):
    orbitals = potential_ref.shape[0]
    count = 512
    for degree in range(1, 5):
        held = walker_ref if degree == 1 else term_ref.at[degree % 2]
        for low in range(0, orbitals, count):
            at = slice(low, low + count)
            next_term = dot(potential_ref[at, :], held[...]) * (1.0 / degree)
            before = walker_ref[at, :].astype(jnp.float32) if degree == 1 else summed_ref[at, :]
            if degree < 4:
                summed_ref[at, :] = before + next_term
                term_ref[(degree + 1) % 2, at, :] = next_term.astype(jnp.bfloat16)
            else:
                out_ref[at, :] = (before + next_term).astype(jnp.bfloat16)


def taylor(potential, walker):
    return pl.pallas_call(
        taylor_kernel,
        in_specs=[WHOLE] * 2,
        out_specs=WHOLE,
        out_shape=jax.ShapeDtypeStruct(walker.shape, jnp.bfloat16),
        scratch_shapes=[
            pltpu.VMEM((2,) + walker.shape, jnp.bfloat16),
            pltpu.VMEM(walker.shape, jnp.float32),
        ],
        compiler_params=params(12),
        cost_estimate=cost(2**31, 2**22),
    )(potential, walker)


def shards(cholesky, walkers, trial_orbitals, fields, log_weights):
    vectors, rows, orbitals = cholesky.shape
    walker_count, _, electrons = walkers.shape
    trial = gather_trial(trial_orbitals)
    phi = exchange(walkers, ROW).reshape(orbitals, electrons)
    part = first_bias(cholesky, trial, walkers)
    weights_now = log_weights
    steps = fields.shape[0]
    for step in range(steps):
        shifted = time_root * row_sum(part, by_permutes=step == 0)
        aux_field = fields[step]
        weights_now = weights_now + jnp.sum(aux_field * shifted - 0.5 * shifted * shifted, axis=1)
        mixed = (aux_field - shifted).astype(jnp.bfloat16)
        sent = potential(mixed, cholesky)
        if step == 0:
            sent, trial, phi = lax.optimization_barrier((sent, trial, phi))
            rotated = rotate(cholesky, trial)
        if step == steps - 1:
            paired = swap(weights_now, "zl")
            sent, paired = lax.optimization_barrier((sent, paired))
        sent = exchange(sent, ROW).reshape(orbitals, orbitals)
        if step == 0:
            sent, rotated = lax.optimization_barrier((sent, rotated))
        phi = taylor(sent, phi)
        if step == steps - 1:
            phi, paired = lax.optimization_barrier((phi, paired))
            paired = jnp.concatenate([weights_now, paired])
            everyone = [paired] + [turn(paired, "y", shift) for shift in range(1, 4)]
            weight_sum = jnp.sum(jnp.exp(jnp.concatenate(everyone)))
            count = walker_count * lax.axis_size(WALK)
            weights_now = weights_now - jnp.log(weight_sum / count)
        phi_rows = exchange(phi.reshape(walker_count, rows, electrons), ROW)
        if step < steps - 1:
            part = bias(rotated, phi_rows)
    return phi_rows, weights_now


def solution(mesh):
    split = Mesh(mesh.devices.reshape(4, 4, 2, 4, 2), ROW + WALK)
    placed = (
        P(None, ROW, None),
        P(WALK, ROW, None),
        P(ROW, None),
        P(None, WALK, None),
        P(WALK),
    )
    return jax.shard_map(
        shards,
        mesh=split,
        in_specs=placed,
        out_specs=(P(WALK, ROW, None), P(WALK)),
        check_vma=False,
    )
```
